32 devices in a mesh: groups: 2 (over y), dp: 16 (over z, x, core).
Axes of the slice: x: 2, y: 2, z: 4, core: 2. Of those that a mesh axis runs over, the one named last changes fastest.
Arguments:
- layer_inputs: bfloat16 [1024, 14336], P(('groups', 'dp')), parts along dimension 0, may hold values from -6 to 6
- output_gradient_rows: bfloat16 [1024, 4096], P(('groups', 'dp')), parts along dimension 0, may hold values from -6 to 6
- eig_in: bfloat16 [14336, 14336], P(None, 'dp'), may hold values from -0.046875 to 0.046875
- eig_out: bfloat16 [4096, 4096], P('dp'), may hold values from -0.09375 to 0.09375
- lengths: int32 [8], P('groups'), parts along dimension 0, may hold values from 1 to 128, 384 in all
Outputs:
- corrections: float32 [28672, 4096], P(('groups', 'dp')), parts along dimension 0
The draws below stay inside these ranges and needn't reach their ends.
There are 2 independent parts, one for each index of `groups`. The reference program is written for one: setup_inputs(seed, part) draws one part's arguments, and reference() takes and returns one part's arrays. A program takes and returns all parts, laid end to end along the dimension named above; an argument that names none is the same for every part. Nothing has to cross between parts.
Inputs may be any that keep to these rules, and one draw needn't show every extreme that they name: `lengths`: each sequence has 128 token slots; slots at or past its length are padding, and some sequence is full.
All inputs are finite; a program needn't handle non-finite values.
Results may differ from the reference program's by a relative error of at most 0.0038.
Values may be sent and summed in bfloat16 or wider, within the bound.
A program may use at most 128 MiB of HBM per device.

```python
import math
import jax
import jax.numpy as jnp
import numpy as np
from jax import lax

DIN = 14336
DOUT = 4096
SEQ_LEN = 128
NSEQ = 4
TOKEN_SLOTS = 512


def strengthened(result, rng, source, target, parts, factor):
    def block_of(position):
        return (jnp.arange(result.shape[position]) // (result.shape[position] // parts)).reshape((-1,) + (1,) * (result.ndim - 1 - position))

    near = jax.random.permutation(rng, parts)[block_of(target)]
    other_side = (block_of(target) + parts // 2) % parts
    return jnp.where((block_of(source) == near) | (block_of(source) == other_side), factor * result, result)


def steps_of(stream_key, shape, split, low, top_value):
    gain, own = 1.0, jax.random.fold_in(stream_key, 6)
    for position, parts in split:
        heights = jnp.exp(jax.random.uniform(jax.random.fold_in(own, position), (parts,), jnp.float32, low / len(split), top_value / len(split)))
        gain = gain * jnp.repeat(heights, shape[position] // parts).reshape([-1 if axis == position else 1 for axis in range(len(shape))])
    return gain


def length_profile(count, total, reach, lean):
    loads = [(1 << 20) // math.isqrt(standing ** lean) + 1 for standing in range(2, count + 1)]
    surplus, counts = total - reach - (count - 1), [1] * (count - 1)
    while surplus > 0:
        movable = [i for i in range(count - 1) if counts[i] < reach]
        whole, remaining = sum([loads[i] for i in movable]), surplus
        for i in movable:
            addition = min(reach - counts[i], max(1, remaining * loads[i] // whole), surplus)
            counts[i] = counts[i] + addition
            surplus = surplus - addition
    return np.array([reach] + counts)


def ragged_sizes(stream_key, count, total, reach, skew):
    if count == 2:
        one = jax.random.randint(stream_key, (), max(1, total - reach), min(reach, total - 1) + 1)
        return jnp.stack([one, total - one])
    sizes = jnp.asarray(length_profile(count, total, reach, skew), jnp.int32)
    twos = (count - 1) // 2
    donor, receiver = sizes[1:1 + 2 * twos:2], sizes[2:2 + 2 * twos:2]
    margin = jnp.minimum(donor - 1, reach - receiver)
    passed = jax.random.randint(jax.random.fold_in(stream_key, 1), (twos,), 0, 1 << 20) % (margin + 1)
    sizes = sizes.at[1:1 + 2 * twos:2].set(donor - passed).at[2:2 + 2 * twos:2].set(receiver + passed)
    return sizes[jax.random.permutation(jax.random.fold_in(stream_key, 2), count)]


def bell_draw(stream_key, extent, spread, bound, split=(), held_as=jnp.bfloat16):
    array = jax.random.normal(stream_key, extent, jnp.float32) * spread
    if len(split) > 0:
        array = steps_of(stream_key, extent, split, -0.22, 0.18) * array
    return jnp.clip(array, min=-bound, max=bound).astype(held_as)


def noise_with(rng, extent, spread, bound, cuts, heavy, kind=jnp.bfloat16):
    entries = spread * jax.random.normal(rng, extent, jnp.float32)
    if cuts:
        entries = entries * steps_of(rng, extent, cuts, -0.22, 0.18)
    return jnp.clip(strengthened(entries, jax.random.fold_in(rng, 3), *heavy), -bound, bound).astype(kind)


def setup_inputs(seed: int = 0, part: int = 0) -> dict:
    seeds = jax.random.split(jax.random.key(seed), 6)
    part_keys = jax.random.split(jax.random.fold_in(seeds[5], part), 6)
    return {
        "layer_inputs": bell_draw(part_keys[0], (TOKEN_SLOTS, DIN), 1.0, 6.0, ((0, 16),)),
        "output_gradient_rows": noise_with(part_keys[1], (TOKEN_SLOTS, DOUT), 1.0, 6.0, ((0, 16),), (1, 0, 16, 2.0)),
        "eig_in": bell_draw(seeds[2], (DIN, DIN), DIN ** -0.5, 0.046875, ((1, 16),)),
        "eig_out": bell_draw(seeds[3], (DOUT, DOUT), DOUT ** -0.5, 0.09375, ((0, 16),)),
        "lengths": ragged_sizes(part_keys[4], NSEQ, 3 * NSEQ * SEQ_LEN // 4, SEQ_LEN, 2).astype(jnp.int32),
    }


def reference(layer_inputs, output_gradient_rows, eig_in, eig_out, lengths):
    slot_index = jnp.arange(SEQ_LEN, dtype=jnp.int32)
    live_mask = slot_index[None, :] < lengths[:, None]
    live_mask = live_mask.reshape(TOKEN_SLOTS, 1)
    input_projection = jnp.dot(layer_inputs, eig_in, preferred_element_type=jnp.float32).astype(jnp.bfloat16)
    input_projection = jnp.where(live_mask, input_projection, jnp.zeros_like(input_projection))
    proj_out = jnp.dot(output_gradient_rows, eig_out, preferred_element_type=jnp.float32).astype(jnp.bfloat16)

    def append_sequence_term(running_total, inputs_pair):
        left_rows, right_side_rows = inputs_pair
        sequence_gradient = jnp.dot(left_rows.T, right_side_rows, preferred_element_type=jnp.float32)
        return running_total + sequence_gradient * sequence_gradient, None

    start_value = jnp.zeros((DIN, DOUT), jnp.float32)
    running_total, _ = lax.scan(append_sequence_term, start_value,
                          (input_projection.reshape(NSEQ, SEQ_LEN, DIN), proj_out.reshape(NSEQ, SEQ_LEN, DOUT)))
    return running_total / (NSEQ * SEQ_LEN)
```

```python
import functools

import jax
import jax.numpy as jnp
from jax import lax
from jax.experimental import pallas as pl
from jax.experimental.pallas import tpu as pltpu
from jax.sharding import PartitionSpec as P

SEQ_LEN = 128
NSEQ = 4
LANES = 2
GROUPS = 4
MESH = pl.DeviceIdType.MESH


def gather_kernel(
    n, x_ref, g_ref, ein_ref, eout_ref, pin_ref, pout_ref,
    xb, gb, pb, eoc, einv, acc,
    barrier_free, loc_sem, ein_sem, eo_send, eo_recv, eo_fwd,
    xs_ring, xr_ring, xs_sib, xr_sib,
    gs_ring, gr_ring, gs_sib, gr_sib,
    ps_ring, pr_ring, ps_sib, pr_sib,
):
    del barrier_free
    chips = n // 2
    side = chips // 2
    grp = lax.axis_index("groups")
    me = lax.axis_index("dp")
    core = lax.rem(me, 2)
    chip = me // 2
    cx = lax.rem(chip, 2)
    cz = chip // 2
    pos = cz * (1 - cx) + (chips - 1 - cz) * cx

    def device_at(position, which_core):
        q = lax.rem(position + 2 * chips, chips)
        qx = q // side
        qz = q * (1 - qx) + (chips - 1 - q) * qx
        return (qz * 2 + qx) * 2 + which_core

    nxt = (device_at(pos + 1, core), device_at(pos - 1, core))
    sib = chip * 2 + (1 - core)

    rows, din = x_ref.shape
    half = rows // 2
    kc = din // (LANES * GROUPS)
    local = []
    for h in range(2):
        local.append(pltpu.make_async_copy(
            g_ref.at[pl.ds(h * half, half)], gb.at[me, h], loc_sem.at[h]))
    for j in range(LANES * GROUPS):
        for h in range(2):
            local.append(pltpu.make_async_copy(
                x_ref.at[pl.ds(h * half, half), pl.ds(j * kc, kc)], xb.at[j, me, h],
                loc_sem.at[2 + j * 2 + h]))
    eh = eout_ref.shape[0] // 2
    ec = eout_ref.shape[1] // n
    nl = 2 + 2 * LANES * GROUPS
    my_rows = pl.ds(pl.multiple_of(grp * eh, 16), eh)
    local.append(pltpu.make_async_copy(
        eout_ref.at[my_rows, pl.ds(pl.multiple_of(me * ec, 128), ec)], eoc.at[me, grp],
        loc_sem.at[nl]))
    for c in local:
        c.start()
    ein_copies = [
        pltpu.make_async_copy(ein_ref.at[pl.ds(j * kc, kc)], einv.at[j], ein_sem.at[j])
        for j in range(LANES * GROUPS)
    ]
    for c in ein_copies:
        c.start()

    barrier = pltpu.get_barrier_semaphore()
    for k in range(1, n):
        pl.semaphore_signal(barrier, inc=1, device_id=(grp, lax.rem(me + k, n)), device_id_type=MESH)
    pl.semaphore_signal(barrier, inc=1, device_id=(1 - grp, me), device_id_type=MESH)
    pl.semaphore_wait(barrier, n)

    for c in local:
        c.wait()

    def eo_copy(k):
        to = lax.rem(me + k, n)
        return pltpu.make_async_remote_copy(
            src_ref=eout_ref.at[my_rows, pl.ds(pl.multiple_of(to * ec, 128), ec)],
            dst_ref=eoc.at[me, grp],
            send_sem=eo_send.at[k], recv_sem=eo_recv.at[k],
            device_id=(grp, to), device_id_type=MESH)

    def ring_copy(item, d, s):
        buf, sends, recvs, _, _ = item
        src = device_at(pos - s if d == 0 else pos + s, core)
        block = buf.at[src, d]
        return pltpu.make_async_remote_copy(
            src_ref=block, dst_ref=block,
            send_sem=sends.at[d, s], recv_sem=recvs.at[d, s],
            device_id=(grp, nxt[d]), device_id_type=MESH)

    def sib_copy(item, d, s):
        buf, _, _, sends, recvs = item
        src = device_at(pos - s if d == 0 else pos + s, core)
        block = buf.at[src, d]
        return pltpu.make_async_remote_copy(
            src_ref=block, dst_ref=block,
            send_sem=sends.at[d, s], recv_sem=recvs.at[d, s],
            device_id=(grp, sib), device_id_type=MESH)

    def wait_ring(item, d, s):
        buf, sends, recvs, _, _ = item
        src = device_at(pos - s - 1 if d == 0 else pos + s + 1, core)
        block = buf.at[src, d]
        pltpu.make_async_remote_copy(
            src_ref=block, dst_ref=block, send_sem=sends.at[d, s], recv_sem=recvs.at[d, s],
            device_id=(grp, nxt[d]), device_id_type=MESH).wait_recv()

    def wait_sib(item, d, s):
        buf, _, _, sends, recvs = item
        src = device_at(pos - s if d == 0 else pos + s, 1 - core)
        block = buf.at[src, d]
        pltpu.make_async_remote_copy(
            src_ref=block, dst_ref=block, send_sem=sends.at[d, s], recv_sem=recvs.at[d, s],
            device_id=(grp, sib), device_id_type=MESH).wait_recv()

    def stage(items, piece=None):
        for item in items:
            for d in range(2):
                ring_copy(item, d, 0).start()
        for item in items:
            for d in range(2):
                sib_copy(item, d, 0).start()

        def hop(s, carry):
            if piece is not None:
                piece(s - 1)
            for item in items:
                for d in range(2):
                    wait_ring(item, d, s - 1)

                    @pl.when(s < chips - 1)
                    def _():
                        ring_copy(item, d, s).start()

                    sib_copy(item, d, s).start()
            return carry

        lax.fori_loop(1, chips, hop, 0)
        if piece is not None:
            piece(chips - 1)

        def finish(s, carry):
            for item in items:
                for d in range(2):
                    wait_sib(item, d, s)
                    sib_copy(item, d, s).wait_send()

                    @pl.when(s < chips - 1)
                    def _():
                        ring_copy(item, d, s).wait_send()
            return carry

        lax.fori_loop(0, chips, finish, 0)

    def x_items(g):
        return [
            (xb.at[g * LANES + w], xs_ring.at[w], xr_ring.at[g, w], xs_sib.at[w], xr_sib.at[g, w])
            for w in range(LANES)
        ]

    tiles = chips // LANES
    per = n // tiles
    mt = per * rows

    def multiply(g, p):
        j = g * LANES + p // tiles
        m = lax.rem(p, tiles)
        lhs = xb[j, pl.ds(m * per, per)].reshape(mt, kc)
        at = pl.ds(pl.multiple_of(m * mt, mt), mt)
        acc[at, :] += jnp.dot(lhs, einv[j], preferred_element_type=jnp.float32)

    g_item = (gb, gs_ring, gr_ring, gs_sib, gr_sib)
    p_item = (pb, ps_ring, pr_ring, ps_sib, pr_sib)

    for k in range(1, n):
        eo_copy(k).start()
    stage([g_item] + x_items(0))

    for k in range(1, n):
        eo_copy(k).wait()
    fwd = pltpu.make_async_remote_copy(
        src_ref=eoc.at[:, grp], dst_ref=eoc.at[:, grp],
        send_sem=eo_fwd.at[0], recv_sem=eo_fwd.at[1],
        device_id=(1 - grp, me), device_id_type=MESH)
    fwd.start()
    acc[...] = jnp.zeros_like(acc)
    for c in ein_copies:
        c.wait()
    fwd.wait()

    def own(m, carry):
        lhs = gb[pl.ds(m * (n // 4), n // 4)].reshape(rows * n // 4, gb.shape[3])
        rhs = eoc[...].reshape(n * 2 * eh, ec)
        res = jnp.dot(lhs, rhs, preferred_element_type=jnp.float32).astype(jnp.bfloat16)
        at = pl.ds(pl.multiple_of(lax.rem(m, 2) * (rows * n // 4), 16), rows * n // 4)
        pb[me, m // 2, at, :] = res
        return carry

    lax.fori_loop(0, 4, own, 0)
    stage([p_item] + x_items(1), functools.partial(multiply, 0))
    out_copy = pltpu.make_async_copy(pb, pout_ref, loc_sem.at[0])
    out_copy.start()

    def group(g, carry):
        stage(x_items(g), functools.partial(multiply, g - 1))
        return carry

    lax.fori_loop(2, GROUPS, group, 0)

    def tail(p, carry):
        multiply(GROUPS - 1, p)
        return carry

    lax.fori_loop(0, chips, tail, 0)
    pin_ref[...] = acc[...].astype(jnp.bfloat16)
    out_copy.wait()


def project(n, x, g, ein, eout):
    rows, din = x.shape
    dout = g.shape[1]
    tokens = rows * n
    cols = ein.shape[1]
    chips = n // 2
    ec = dout // n
    nchunk = LANES * GROUPS
    kc = din // nchunk
    dma = pltpu.SemaphoreType.DMA
    ring = (2, chips - 1)
    sib = (2, chips)
    return pl.pallas_call(
        functools.partial(gather_kernel, n),
        out_shape=(
            jax.ShapeDtypeStruct((tokens, cols), jnp.bfloat16),
            jax.ShapeDtypeStruct((n, 2, tokens // 2, ec), jnp.bfloat16),
        ),
        in_specs=[pl.BlockSpec(memory_space=pl.ANY)] * 4,
        out_specs=(
            pl.BlockSpec(memory_space=pltpu.VMEM),
            pl.BlockSpec(memory_space=pl.ANY),
        ),
        scratch_shapes=[
            pltpu.VMEM((nchunk, n, 2, rows // 2, kc), jnp.bfloat16),
            pltpu.VMEM((n, 2, rows // 2, dout), jnp.bfloat16),
            pltpu.VMEM((n, 2, tokens // 2, ec), jnp.bfloat16),
            pltpu.VMEM((n, 2, eout.shape[0] // 2, ec), jnp.bfloat16),
            pltpu.VMEM((nchunk, kc, cols), jnp.bfloat16),
            pltpu.VMEM((tokens, cols), jnp.float32),
            pltpu.SemaphoreType.REGULAR,
            dma((3 + 2 * nchunk,)),
            dma((nchunk,)),
            dma((n,)),
            dma((n,)),
            dma((2,)),
            dma((LANES,) + ring), dma((GROUPS, LANES) + ring),
            dma((LANES,) + sib), dma((GROUPS, LANES) + sib),
            dma(ring), dma(ring), dma(sib), dma(sib),
            dma(ring), dma(ring), dma(sib), dma(sib),
        ],
        compiler_params=pltpu.CompilerParams(
            collective_id=0, has_side_effects=True, vmem_limit_bytes=60 * 1024 * 1024
        ),
        cost_estimate=pl.CostEstimate(
            flops=2 * tokens * (din * cols + dout * ec),
            bytes_accessed=2 * din * cols, transcendentals=0),
    )(x, g, ein, eout)


def correction_kernel(seq_len, nseq, len_ref, pin_ref, p_ref, out_ref, left):
    @pl.when(pl.program_id(0) == 0)
    def _():
        for s in range(nseq):
            block = pin_ref[pl.ds(s * seq_len, seq_len), :].astype(jnp.float32)
            slot = lax.broadcasted_iota(jnp.int32, block.shape, 0)
            block = jnp.where(slot < len_ref[s], block, 0.0)
            left[s] = block.T.astype(jnp.bfloat16)

    total = None
    for s in range(nseq):
        grad = jnp.dot(
            left[s], p_ref[0, pl.ds(s * seq_len, seq_len), :], preferred_element_type=jnp.float32
        )
        total = grad * grad if total is None else total + grad * grad
    out_ref[...] = total * (1.0 / (nseq * seq_len))


def correct(pin, p, lengths):
    n, tokens, ec = p.shape
    cols = pin.shape[1]
    return pl.pallas_call(
        functools.partial(correction_kernel, SEQ_LEN, NSEQ),
        grid=(n,),
        out_shape=jax.ShapeDtypeStruct((cols, n * ec), jnp.float32),
        in_specs=[
            pl.BlockSpec(memory_space=pltpu.SMEM),
            pl.BlockSpec((tokens, cols), lambda i: (0, 0)),
            pl.BlockSpec((1, tokens, ec), lambda i: (i, 0, 0)),
        ],
        out_specs=pl.BlockSpec((cols, ec), lambda i: (0, i)),
        scratch_shapes=[pltpu.VMEM((NSEQ, cols, SEQ_LEN), jnp.bfloat16)],
        compiler_params=pltpu.CompilerParams(vmem_limit_bytes=40 * 1024 * 1024),
    )(lengths, pin, p)


def on_device_kernels(n, x, g, ein, eout, lengths):
    pin, p = project(n, x, g, ein, eout)
    return correct(pin, p.reshape(n, p.shape[1] * p.shape[2], p.shape[3]), lengths)


def on_device(layer_inputs, output_gradient_rows, eig_in, eig_out, lengths):
    input_projection = jnp.dot(
        lax.all_gather(layer_inputs, "dp", axis=0, tiled=True),
        eig_in,
        preferred_element_type=jnp.float32,
    ).astype(jnp.bfloat16)
    slot_index = jnp.arange(SEQ_LEN, dtype=jnp.int32)
    live_mask = slot_index[None, :] < lengths[:, None]
    input_projection = input_projection.reshape(NSEQ, SEQ_LEN, input_projection.shape[1])
    input_projection = jnp.where(
        live_mask[:, :, None], input_projection, jnp.zeros_like(input_projection)
    )
    out_basis = lax.all_to_all(eig_out, "dp", split_axis=1, concat_axis=0, tiled=True)
    own_columns = jnp.dot(
        lax.all_gather(output_gradient_rows, "dp", axis=0, tiled=True),
        out_basis,
        preferred_element_type=jnp.float32,
    ).astype(jnp.bfloat16)
    projected = lax.all_gather(own_columns, "dp", axis=1, tiled=True)
    right_side_rows = projected.reshape(NSEQ, SEQ_LEN, projected.shape[1])
    sequence_gradient = jnp.einsum(
        "fer,feq->frq", input_projection, right_side_rows, preferred_element_type=jnp.float32
    )
    return jnp.sum(sequence_gradient * sequence_gradient, axis=0) / (NSEQ * SEQ_LEN)


def solution(mesh):
    placed = (
        P(("groups", "dp"), None),
        P(("groups", "dp"), None),
        P(None, "dp"),
        P("dp", None),
        P("groups"),
    )
    n = mesh.shape["dp"]
    if mesh.shape["groups"] == 2 and n == 16:
        body = functools.partial(on_device_kernels, n)
    else:
        body = on_device
    return jax.shard_map(
        body, mesh=mesh, in_specs=placed, out_specs=P(("groups", "dp"), None), check_vma=False
    )
```

```python
import functools

import jax
import jax.numpy as jnp
from jax import lax
from jax.experimental import pallas as pl
from jax.experimental.pallas import tpu as pltpu
from jax.sharding import PartitionSpec as P

SEQ_LEN = 128
NSEQ = 4
LANES = 4
GROUPS = 2
MESH = pl.DeviceIdType.MESH


def gather_kernel(
    n, x_ref, g_ref, ein_ref, eout_ref, pin_ref, pout_ref,
    xb, gb, pb, eoc, einv, acc,
    barrier_free, loc_sem, ein_sem, eo_send, eo_recv, fwd_send, fwd_recv,
    xs_ring, xr_ring, xs_sib, xr_sib,
    gs_ring, gr_ring, gs_sib, gr_sib,
    ps_ring, pr_ring, ps_sib, pr_sib,
):
    del barrier_free
    chips = n // 2
    side = chips // 2
    grp = lax.axis_index("groups")
    me = lax.axis_index("dp")
    core = lax.rem(me, 2)
    chip = me // 2
    cx = lax.rem(chip, 2)
    cz = chip // 2
    pos = cz * (1 - cx) + (chips - 1 - cz) * cx

    def device_at(position, which_core):
        q = lax.rem(position + 2 * chips, chips)
        qx = q // side
        qz = q * (1 - qx) + (chips - 1 - q) * qx
        return (qz * 2 + qx) * 2 + which_core

    nxt = (device_at(pos + 1, core), device_at(pos - 1, core))
    sib = chip * 2 + (1 - core)

    rows, din = x_ref.shape
    half = rows // 2
    kc = din // (LANES * GROUPS)
    local = []
    for h in range(2):
        local.append(pltpu.make_async_copy(
            g_ref.at[pl.ds(h * half, half)], gb.at[me, h], loc_sem.at[h]))
    for j in range(LANES * GROUPS):
        for h in range(2):
            local.append(pltpu.make_async_copy(
                x_ref.at[pl.ds(h * half, half), pl.ds(j * kc, kc)], xb.at[j, me, h],
                loc_sem.at[2 + j * 2 + h]))
    eh = eout_ref.shape[0] // 2
    ec = eout_ref.shape[1] // n
    nl = 2 + 2 * LANES * GROUPS
    my_rows = pl.ds(pl.multiple_of(grp * eh, 16), eh)
    local.append(pltpu.make_async_copy(
        eout_ref.at[my_rows, pl.ds(pl.multiple_of(me * ec, 128), ec)], eoc.at[me, grp],
        loc_sem.at[nl]))
    for c in local:
        c.start()
    ein_copies = [
        pltpu.make_async_copy(ein_ref.at[pl.ds(j * kc, kc)], einv.at[j], ein_sem.at[j])
        for j in range(LANES * GROUPS)
    ]
    for c in ein_copies:
        c.start()

    barrier = pltpu.get_barrier_semaphore()
    for k in range(1, n):
        pl.semaphore_signal(barrier, inc=1, device_id=(grp, lax.rem(me + k, n)), device_id_type=MESH)
    pl.semaphore_signal(barrier, inc=1, device_id=(1 - grp, me), device_id_type=MESH)
    pl.semaphore_wait(barrier, n)

    for c in local:
        c.wait()

    def eo_copy(k):
        to = lax.rem(me + k, n)
        return pltpu.make_async_remote_copy(
            src_ref=eout_ref.at[my_rows, pl.ds(pl.multiple_of(to * ec, 128), ec)],
            dst_ref=eoc.at[me, grp],
            send_sem=eo_send.at[k], recv_sem=eo_recv.at[k],
            device_id=(grp, to), device_id_type=MESH)

    def ring_copy(item, d, s):
        buf, sends, recvs, _, _ = item
        src = device_at(pos - s if d == 0 else pos + s, core)
        block = buf.at[src, d]
        return pltpu.make_async_remote_copy(
            src_ref=block, dst_ref=block,
            send_sem=sends.at[d, s], recv_sem=recvs.at[d, s],
            device_id=(grp, nxt[d]), device_id_type=MESH)

    def sib_copy(item, d, s):
        buf, _, _, sends, recvs = item
        src = device_at(pos - s if d == 0 else pos + s, core)
        block = buf.at[src, d]
        return pltpu.make_async_remote_copy(
            src_ref=block, dst_ref=block,
            send_sem=sends.at[d, s], recv_sem=recvs.at[d, s],
            device_id=(grp, sib), device_id_type=MESH)

    def wait_ring(item, d, s):
        buf, sends, recvs, _, _ = item
        src = device_at(pos - s - 1 if d == 0 else pos + s + 1, core)
        block = buf.at[src, d]
        pltpu.make_async_remote_copy(
            src_ref=block, dst_ref=block, send_sem=sends.at[d, s], recv_sem=recvs.at[d, s],
            device_id=(grp, nxt[d]), device_id_type=MESH).wait_recv()

    def wait_sib(item, d, s):
        buf, _, _, sends, recvs = item
        src = device_at(pos - s if d == 0 else pos + s, 1 - core)
        block = buf.at[src, d]
        pltpu.make_async_remote_copy(
            src_ref=block, dst_ref=block, send_sem=sends.at[d, s], recv_sem=recvs.at[d, s],
            device_id=(grp, sib), device_id_type=MESH).wait_recv()

    def begin(items):
        for item in items:
            for d in range(2):
                ring_copy(item, d, 0).start()
        for item in items:
            for d in range(2):
                sib_copy(item, d, 0).start()

    def stage(items, piece=None, last=None):
        def hop(s, carry):
            if piece is not None:
                piece(s - 1)
            for item in items:
                for d in range(2):
                    wait_ring(item, d, s - 1)

                    @pl.when(s < chips - 1)
                    def _():
                        ring_copy(item, d, s).start()

                    sib_copy(item, d, s).start()
            return carry

        lax.fori_loop(1, chips, hop, 0)
        if last is not None:
            last(chips - 1)

        def finish(s, carry):
            for item in items:
                for d in range(2):
                    wait_sib(item, d, s)
                    sib_copy(item, d, s).wait_send()

                    @pl.when(s < chips - 1)
                    def _():
                        ring_copy(item, d, s).wait_send()
            return carry

        lax.fori_loop(0, chips, finish, 0)

    def x_items(g):
        return [
            (xb.at[g * LANES + w], xs_ring.at[w], xr_ring.at[g, w], xs_sib.at[w], xr_sib.at[g, w])
            for w in range(LANES)
        ]

    tiles = chips // LANES
    per = n // tiles
    mt = per * rows

    def multiply(g, p):
        j = g * LANES + p // tiles
        m = lax.rem(p, tiles)
        lhs = xb[j, pl.ds(m * per, per)].reshape(mt, kc)
        at = pl.ds(pl.multiple_of(m * mt, 128), mt)
        acc[at, :] += jnp.dot(lhs, einv[j], preferred_element_type=jnp.float32)

    g_item = (gb, gs_ring, gr_ring, gs_sib, gr_sib)
    p_item = (pb, ps_ring, pr_ring, ps_sib, pr_sib)

    def fwd_copy(k, part):
        src = lax.rem(me - k + n, n)
        return pltpu.make_async_remote_copy(
            src_ref=eoc.at[src, part], dst_ref=eoc.at[src, part],
            send_sem=fwd_send.at[k], recv_sem=fwd_recv.at[k],
            device_id=(1 - grp, me), device_id_type=MESH)

    def hand_on(s):
        for k in (2 * s + 1, 2 * s + 2):
            eo_copy(k).wait()
            fwd_copy(k, grp).start()

    fwd_copy(0, grp).start()
    begin([g_item])
    for k in range(1, n):
        eo_copy(k).start()
    begin(x_items(0))
    stage([g_item] + x_items(0), hand_on)
    eo_copy(n - 1).wait()
    fwd_copy(n - 1, grp).start()

    begin(x_items(1))
    acc[...] = jnp.zeros_like(acc)
    for c in ein_copies:
        c.wait()
    for k in range(n):
        fwd_copy(k, grp).wait_send()
        fwd_copy(k, 1 - grp).wait_recv()

    def own(m, carry):
        lhs = gb[pl.ds(m * (n // 4), n // 4)].reshape(rows * n // 4, gb.shape[3])
        rhs = eoc[...].reshape(n * 2 * eh, ec)
        res = jnp.dot(lhs, rhs, preferred_element_type=jnp.float32).astype(jnp.bfloat16)
        at = pl.ds(pl.multiple_of(lax.rem(m, 2) * (rows * n // 4), 16), rows * n // 4)
        pb[me, m // 2, at, :] = res
        return carry

    lax.fori_loop(0, 4, own, 0)
    begin([p_item])
    piece = functools.partial(multiply, 0)
    stage([p_item] + x_items(1), piece, piece)
    out_copy = pltpu.make_async_copy(pb, pout_ref, loc_sem.at[0])
    out_copy.start()

    def tail(p, carry):
        multiply(GROUPS - 1, p)
        return carry

    lax.fori_loop(0, chips, tail, 0)
    pin_ref[...] = acc[...].astype(jnp.bfloat16)
    out_copy.wait()


def project(n, x, g, ein, eout):
    rows, din = x.shape
    dout = g.shape[1]
    tokens = rows * n
    cols = ein.shape[1]
    chips = n // 2
    ec = dout // n
    nchunk = LANES * GROUPS
    kc = din // nchunk
    dma = pltpu.SemaphoreType.DMA
    ring = (2, chips - 1)
    sib = (2, chips)
    return pl.pallas_call(
        functools.partial(gather_kernel, n),
        out_shape=(
            jax.ShapeDtypeStruct((tokens, cols), jnp.bfloat16),
            jax.ShapeDtypeStruct((n, 2, tokens // 2, ec), jnp.bfloat16),
        ),
        in_specs=[pl.BlockSpec(memory_space=pl.ANY)] * 4,
        out_specs=(
            pl.BlockSpec(memory_space=pltpu.VMEM),
            pl.BlockSpec(memory_space=pl.ANY),
        ),
        scratch_shapes=[
            pltpu.VMEM((nchunk, n, 2, rows // 2, kc), jnp.bfloat16),
            pltpu.VMEM((n, 2, rows // 2, dout), jnp.bfloat16),
            pltpu.VMEM((n, 2, tokens // 2, ec), jnp.bfloat16),
            pltpu.VMEM((n, 2, eout.shape[0] // 2, ec), jnp.bfloat16),
            pltpu.VMEM((nchunk, kc, cols), jnp.bfloat16),
            pltpu.VMEM((tokens, cols), jnp.float32),
            pltpu.SemaphoreType.REGULAR,
            dma((3 + 2 * nchunk,)),
            dma((nchunk,)),
            dma((n,)),
            dma((n,)),
            dma((n,)),
            dma((n,)),
            dma((LANES,) + ring), dma((GROUPS, LANES) + ring),
            dma((LANES,) + sib), dma((GROUPS, LANES) + sib),
            dma(ring), dma(ring), dma(sib), dma(sib),
            dma(ring), dma(ring), dma(sib), dma(sib),
        ],
        compiler_params=pltpu.CompilerParams(
            collective_id=0, has_side_effects=True, vmem_limit_bytes=60 * 1024 * 1024
        ),
        cost_estimate=pl.CostEstimate(
            flops=2 * tokens * (din * cols + dout * ec),
            bytes_accessed=2 * din * cols, transcendentals=0),
    )(x, g, ein, eout)


def correction_kernel(seq_len, nseq, len_ref, pin_ref, p_ref, out_ref, left):
    @pl.when(pl.program_id(0) == 0)
    def _():
        for s in range(nseq):
            block = pin_ref[pl.ds(s * seq_len, seq_len), :].astype(jnp.float32)
            slot = lax.broadcasted_iota(jnp.int32, block.shape, 0)
            block = jnp.where(slot < len_ref[s], block, 0.0)
            left[s] = block.T.astype(jnp.bfloat16)

    total = None
    for s in range(nseq):
        grad = jnp.dot(
            left[s], p_ref[0, pl.ds(s * seq_len, seq_len), :], preferred_element_type=jnp.float32
        )
        total = grad * grad if total is None else total + grad * grad
    out_ref[...] = total * (1.0 / (nseq * seq_len))


def correct(pin, p, lengths):
    n, tokens, ec = p.shape
    cols = pin.shape[1]
    return pl.pallas_call(
        functools.partial(correction_kernel, SEQ_LEN, NSEQ),
        grid=(n,),
        out_shape=jax.ShapeDtypeStruct((cols, n * ec), jnp.float32),
        in_specs=[
            pl.BlockSpec(memory_space=pltpu.SMEM),
            pl.BlockSpec((tokens, cols), lambda i: (0, 0)),
            pl.BlockSpec((1, tokens, ec), lambda i: (i, 0, 0)),
        ],
        out_specs=pl.BlockSpec((cols, ec), lambda i: (0, i)),
        scratch_shapes=[pltpu.VMEM((NSEQ, cols, SEQ_LEN), jnp.bfloat16)],
        compiler_params=pltpu.CompilerParams(vmem_limit_bytes=40 * 1024 * 1024),
    )(lengths, pin, p)


def on_device_kernels(n, x, g, ein, eout, lengths):
    pin, p = project(n, x, g, ein, eout)
    return correct(pin, p.reshape(n, p.shape[1] * p.shape[2], p.shape[3]), lengths)


def on_device(layer_inputs, output_gradient_rows, eig_in, eig_out, lengths):
    input_projection = jnp.dot(
        lax.all_gather(layer_inputs, "dp", axis=0, tiled=True),
        eig_in,
        preferred_element_type=jnp.float32,
    ).astype(jnp.bfloat16)
    slot_index = jnp.arange(SEQ_LEN, dtype=jnp.int32)
    live_mask = slot_index[None, :] < lengths[:, None]
    input_projection = input_projection.reshape(NSEQ, SEQ_LEN, input_projection.shape[1])
    input_projection = jnp.where(
        live_mask[:, :, None], input_projection, jnp.zeros_like(input_projection)
    )
    out_basis = lax.all_to_all(eig_out, "dp", split_axis=1, concat_axis=0, tiled=True)
    own_columns = jnp.dot(
        lax.all_gather(output_gradient_rows, "dp", axis=0, tiled=True),
        out_basis,
        preferred_element_type=jnp.float32,
    ).astype(jnp.bfloat16)
    projected = lax.all_gather(own_columns, "dp", axis=1, tiled=True)
    right_side_rows = projected.reshape(NSEQ, SEQ_LEN, projected.shape[1])
    sequence_gradient = jnp.einsum(
        "fer,feq->frq", input_projection, right_side_rows, preferred_element_type=jnp.float32
    )
    return jnp.sum(sequence_gradient * sequence_gradient, axis=0) / (NSEQ * SEQ_LEN)


def solution(mesh):
    placed = (
        P(("groups", "dp"), None),
        P(("groups", "dp"), None),
        P(None, "dp"),
        P("dp", None),
        P("groups"),
    )
    n = mesh.shape["dp"]
    if mesh.shape["groups"] == 2 and n == 16:
        body = functools.partial(on_device_kernels, n)
    else:
        body = on_device
    return jax.shard_map(
        body, mesh=mesh, in_specs=placed, out_specs=P(("groups", "dp"), None), check_vma=False
    )
```

```python
import functools

import jax
import jax.numpy as jnp
from jax import lax
from jax.experimental import pallas as pl
from jax.experimental.pallas import tpu as pltpu
from jax.sharding import PartitionSpec as P

SEQ_LEN = 128
NSEQ = 4
LANES = 4
GROUPS = 2
MESH = pl.DeviceIdType.MESH


def gather_kernel(
    n, x_ref, g_ref, ein_ref, eout_ref, pin_ref, pout_ref,
    xb, gb, pb, eoc, einv, acc,
    barrier_free, loc_sem, ein_sem, eo_send, eo_recv, fwd_send, fwd_recv,
    xs_ring, xr_ring, xs_sib, xr_sib,
    gs_ring, gr_ring, gs_sib, gr_sib,
    ps_ring, pr_ring, ps_sib, pr_sib,
):
    del barrier_free
    chips = n // 2
    side = chips // 2
    grp = lax.axis_index("groups")
    me = lax.axis_index("dp")
    core = lax.rem(me, 2)
    chip = me // 2
    cx = lax.rem(chip, 2)
    cz = chip // 2
    pos = cz * (1 - cx) + (chips - 1 - cz) * cx

    def device_at(position, which_core):
        q = lax.rem(position + 2 * chips, chips)
        qx = q // side
        qz = q * (1 - qx) + (chips - 1 - q) * qx
        return (qz * 2 + qx) * 2 + which_core

    nxt = (device_at(pos + 1, core), device_at(pos - 1, core))
    sib = chip * 2 + (1 - core)

    rows, din = x_ref.shape
    half = rows // 2
    kc = din // (LANES * GROUPS)
    local = []
    for h in range(2):
        local.append(pltpu.make_async_copy(
            g_ref.at[pl.ds(h * half, half)], gb.at[me, h], loc_sem.at[h]))
    for j in range(LANES * GROUPS):
        for h in range(2):
            local.append(pltpu.make_async_copy(
                x_ref.at[pl.ds(h * half, half), pl.ds(j * kc, kc)], xb.at[j, me, h],
                loc_sem.at[2 + j * 2 + h]))
    eh = eout_ref.shape[0] // 2
    ec = eout_ref.shape[1] // n
    nl = 2 + 2 * LANES * GROUPS
    my_rows = pl.ds(pl.multiple_of(grp * eh, 16), eh)
    local.append(pltpu.make_async_copy(
        eout_ref.at[my_rows, pl.ds(pl.multiple_of(me * ec, 128), ec)], eoc.at[me, grp],
        loc_sem.at[nl]))
    for c in local:
        c.start()
    ein_copies = [
        pltpu.make_async_copy(ein_ref.at[pl.ds(j * kc, kc)], einv.at[j], ein_sem.at[j])
        for j in range(LANES * GROUPS)
    ]
    for c in ein_copies:
        c.start()

    barrier = pltpu.get_barrier_semaphore()
    for k in range(1, n):
        pl.semaphore_signal(barrier, inc=1, device_id=(grp, lax.rem(me + k, n)), device_id_type=MESH)
    pl.semaphore_signal(barrier, inc=1, device_id=(1 - grp, me), device_id_type=MESH)
    pl.semaphore_wait(barrier, n)

    for c in local:
        c.wait()

    def eo_copy(k):
        to = lax.rem(me + k, n)
        return pltpu.make_async_remote_copy(
            src_ref=eout_ref.at[my_rows, pl.ds(pl.multiple_of(to * ec, 128), ec)],
            dst_ref=eoc.at[me, grp],
            send_sem=eo_send.at[k], recv_sem=eo_recv.at[k],
            device_id=(grp, to), device_id_type=MESH)

    def ring_copy(item, d, s):
        buf, sends, recvs, _, _ = item
        src = device_at(pos - s if d == 0 else pos + s, core)
        block = buf.at[src, d]
        return pltpu.make_async_remote_copy(
            src_ref=block, dst_ref=block,
            send_sem=sends.at[d, s], recv_sem=recvs.at[d, s],
            device_id=(grp, nxt[d]), device_id_type=MESH)

    def sib_copy(item, d, s):
        buf, _, _, sends, recvs = item
        src = device_at(pos - s if d == 0 else pos + s, core)
        block = buf.at[src, d]
        return pltpu.make_async_remote_copy(
            src_ref=block, dst_ref=block,
            send_sem=sends.at[d, s], recv_sem=recvs.at[d, s],
            device_id=(grp, sib), device_id_type=MESH)

    def wait_ring(item, d, s):
        buf, sends, recvs, _, _ = item
        src = device_at(pos - s - 1 if d == 0 else pos + s + 1, core)
        block = buf.at[src, d]
        pltpu.make_async_remote_copy(
            src_ref=block, dst_ref=block, send_sem=sends.at[d, s], recv_sem=recvs.at[d, s],
            device_id=(grp, nxt[d]), device_id_type=MESH).wait_recv()

    def wait_sib(item, d, s):
        buf, _, _, sends, recvs = item
        src = device_at(pos - s if d == 0 else pos + s, 1 - core)
        block = buf.at[src, d]
        pltpu.make_async_remote_copy(
            src_ref=block, dst_ref=block, send_sem=sends.at[d, s], recv_sem=recvs.at[d, s],
            device_id=(grp, sib), device_id_type=MESH).wait_recv()

    def begin(items):
        for item in items:
            for d in range(2):
                ring_copy(item, d, 0).start()
        for item in items:
            for d in range(2):
                sib_copy(item, d, 0).start()

    def stage(items, piece=None, last=None):
        def hop(s, carry):
            if piece is not None:
                piece(s - 1)
            for item in items:
                for d in range(2):
                    wait_ring(item, d, s - 1)

                    @pl.when(s < chips - 1)
                    def _():
                        ring_copy(item, d, s).start()

                    sib_copy(item, d, s).start()
            return carry

        lax.fori_loop(1, chips, hop, 0)
        if last is not None:
            last(chips - 1)

        def finish(s, carry):
            for item in items:
                for d in range(2):
                    wait_sib(item, d, s)
                    sib_copy(item, d, s).wait_send()

                    @pl.when(s < chips - 1)
                    def _():
                        ring_copy(item, d, s).wait_send()
            return carry

        lax.fori_loop(0, chips, finish, 0)

    def x_items(g):
        return [
            (xb.at[g * LANES + w], xs_ring.at[g, w], xr_ring.at[g, w], xs_sib.at[g, w], xr_sib.at[g, w])
            for w in range(LANES)
        ]

    tiles = chips // LANES
    per = n // tiles
    mt = per * rows

    def multiply(g, p):
        j = g * LANES + p // tiles
        m = lax.rem(p, tiles)
        lhs = xb[j, pl.ds(m * per, per)].reshape(mt, kc)
        at = pl.ds(pl.multiple_of(m * mt, 128), mt)
        acc[at, :] += jnp.dot(lhs, einv[j], preferred_element_type=jnp.float32)

    g_item = (gb, gs_ring, gr_ring, gs_sib, gr_sib)
    p_item = (pb, ps_ring, pr_ring, ps_sib, pr_sib)

    def fwd_copy(k, part):
        src = lax.rem(me - k + n, n)
        return pltpu.make_async_remote_copy(
            src_ref=eoc.at[src, part], dst_ref=eoc.at[src, part],
            send_sem=fwd_send.at[k], recv_sem=fwd_recv.at[k],
            device_id=(1 - grp, me), device_id_type=MESH)

    def hand_on(s):
        for k in (2 * s + 1, 2 * s + 2):
            eo_copy(k).wait()
            fwd_copy(k, grp).start()

        @pl.when(s == chips - 3)
        def _():
            begin(x_items(1))

    fwd_copy(0, grp).start()
    begin([g_item])
    for k in range(1, n):
        eo_copy(k).start()
    begin(x_items(0))
    stage([g_item] + x_items(0), hand_on)
    eo_copy(n - 1).wait()
    fwd_copy(n - 1, grp).start()

    acc[...] = jnp.zeros_like(acc)
    for c in ein_copies:
        c.wait()
    for k in range(n):
        fwd_copy(k, grp).wait_send()
        fwd_copy(k, 1 - grp).wait_recv()

    def own(m, carry):
        lhs = gb[pl.ds(m * (n // 4), n // 4)].reshape(rows * n // 4, gb.shape[3])
        rhs = eoc[...].reshape(n * 2 * eh, ec)
        res = jnp.dot(lhs, rhs, preferred_element_type=jnp.float32).astype(jnp.bfloat16)
        at = pl.ds(pl.multiple_of(lax.rem(m, 2) * (rows * n // 4), 16), rows * n // 4)
        pb[me, m // 2, at, :] = res
        return carry

    lax.fori_loop(0, 4, own, 0)
    begin([p_item])
    piece = functools.partial(multiply, 0)
    stage([p_item] + x_items(1), piece, piece)
    out_copy = pltpu.make_async_copy(pb, pout_ref, loc_sem.at[0])
    out_copy.start()

    def tail(p, carry):
        multiply(GROUPS - 1, p)
        return carry

    lax.fori_loop(0, chips, tail, 0)
    pin_ref[...] = acc[...].astype(jnp.bfloat16)
    out_copy.wait()


def project(n, x, g, ein, eout):
    rows, din = x.shape
    dout = g.shape[1]
    tokens = rows * n
    cols = ein.shape[1]
    chips = n // 2
    ec = dout // n
    nchunk = LANES * GROUPS
    kc = din // nchunk
    dma = pltpu.SemaphoreType.DMA
    ring = (2, chips - 1)
    sib = (2, chips)
    return pl.pallas_call(
        functools.partial(gather_kernel, n),
        out_shape=(
            jax.ShapeDtypeStruct((tokens, cols), jnp.bfloat16),
            jax.ShapeDtypeStruct((n, 2, tokens // 2, ec), jnp.bfloat16),
        ),
        in_specs=[pl.BlockSpec(memory_space=pl.ANY)] * 4,
        out_specs=(
            pl.BlockSpec(memory_space=pltpu.VMEM),
            pl.BlockSpec(memory_space=pl.ANY),
        ),
        scratch_shapes=[
            pltpu.VMEM((nchunk, n, 2, rows // 2, kc), jnp.bfloat16),
            pltpu.VMEM((n, 2, rows // 2, dout), jnp.bfloat16),
            pltpu.VMEM((n, 2, tokens // 2, ec), jnp.bfloat16),
            pltpu.VMEM((n, 2, eout.shape[0] // 2, ec), jnp.bfloat16),
            pltpu.VMEM((nchunk, kc, cols), jnp.bfloat16),
            pltpu.VMEM((tokens, cols), jnp.float32),
            pltpu.SemaphoreType.REGULAR,
            dma((3 + 2 * nchunk,)),
            dma((nchunk,)),
            dma((n,)),
            dma((n,)),
            dma((n,)),
            dma((n,)),
            dma((GROUPS, LANES) + ring), dma((GROUPS, LANES) + ring),
            dma((GROUPS, LANES) + sib), dma((GROUPS, LANES) + sib),
            dma(ring), dma(ring), dma(sib), dma(sib),
            dma(ring), dma(ring), dma(sib), dma(sib),
        ],
        compiler_params=pltpu.CompilerParams(
            collective_id=0, has_side_effects=True, vmem_limit_bytes=60 * 1024 * 1024
        ),
        cost_estimate=pl.CostEstimate(
            flops=2 * tokens * (din * cols + dout * ec),
            bytes_accessed=2 * din * cols, transcendentals=0),
    )(x, g, ein, eout)


def correction_kernel(seq_len, nseq, len_ref, pin_ref, p_ref, out_ref, left):
    @pl.when(pl.program_id(0) == 0)
    def _():
        for s in range(nseq):
            block = pin_ref[pl.ds(s * seq_len, seq_len), :].astype(jnp.float32)
            slot = lax.broadcasted_iota(jnp.int32, block.shape, 0)
            block = jnp.where(slot < len_ref[s], block, 0.0)
            left[s] = block.T.astype(jnp.bfloat16)

    total = None
    for s in range(nseq):
        grad = jnp.dot(
            left[s], p_ref[0, pl.ds(s * seq_len, seq_len), :], preferred_element_type=jnp.float32
        )
        total = grad * grad if total is None else total + grad * grad
    out_ref[...] = total * (1.0 / (nseq * seq_len))


def correct(pin, p, lengths):
    n, tokens, ec = p.shape
    cols = pin.shape[1]
    return pl.pallas_call(
        functools.partial(correction_kernel, SEQ_LEN, NSEQ),
        grid=(n,),
        out_shape=jax.ShapeDtypeStruct((cols, n * ec), jnp.float32),
        in_specs=[
            pl.BlockSpec(memory_space=pltpu.SMEM),
            pl.BlockSpec((tokens, cols), lambda i: (0, 0)),
            pl.BlockSpec((1, tokens, ec), lambda i: (i, 0, 0)),
        ],
        out_specs=pl.BlockSpec((cols, ec), lambda i: (0, i)),
        scratch_shapes=[pltpu.VMEM((NSEQ, cols, SEQ_LEN), jnp.bfloat16)],
        compiler_params=pltpu.CompilerParams(vmem_limit_bytes=60 * 1024 * 1024),
    )(lengths, pin, p)


def on_device_kernels(n, x, g, ein, eout, lengths):
    pin, p = project(n, x, g, ein, eout)
    return correct(pin, p.reshape(n, p.shape[1] * p.shape[2], p.shape[3]), lengths)


def on_device(layer_inputs, output_gradient_rows, eig_in, eig_out, lengths):
    input_projection = jnp.dot(
        lax.all_gather(layer_inputs, "dp", axis=0, tiled=True),
        eig_in,
        preferred_element_type=jnp.float32,
    ).astype(jnp.bfloat16)
    slot_index = jnp.arange(SEQ_LEN, dtype=jnp.int32)
    live_mask = slot_index[None, :] < lengths[:, None]
    input_projection = input_projection.reshape(NSEQ, SEQ_LEN, input_projection.shape[1])
    input_projection = jnp.where(
        live_mask[:, :, None], input_projection, jnp.zeros_like(input_projection)
    )
    out_basis = lax.all_to_all(eig_out, "dp", split_axis=1, concat_axis=0, tiled=True)
    own_columns = jnp.dot(
        lax.all_gather(output_gradient_rows, "dp", axis=0, tiled=True),
        out_basis,
        preferred_element_type=jnp.float32,
    ).astype(jnp.bfloat16)
    projected = lax.all_gather(own_columns, "dp", axis=1, tiled=True)
    right_side_rows = projected.reshape(NSEQ, SEQ_LEN, projected.shape[1])
    sequence_gradient = jnp.einsum(
        "fer,feq->frq", input_projection, right_side_rows, preferred_element_type=jnp.float32
    )
    return jnp.sum(sequence_gradient * sequence_gradient, axis=0) / (NSEQ * SEQ_LEN)


def solution(mesh):
    placed = (
        P(("groups", "dp"), None),
        P(("groups", "dp"), None),
        P(None, "dp"),
        P("dp", None),
        P("groups"),
    )
    n = mesh.shape["dp"]
    if mesh.shape["groups"] == 2 and n == 16:
        body = functools.partial(on_device_kernels, n)
    else:
        body = on_device
    return jax.shard_map(
        body, mesh=mesh, in_specs=placed, out_specs=P(("groups", "dp"), None), check_vma=False
    )
```
